256 devices in a mesh: dp: 16 (over x_hi, z), tensor: 16 (over x_lo, y, core).
Axes of the slice: x: 4 (x_hi: 2, x_lo: 2; x = x_hi * 2 + x_lo), y: 4, z: 8, core: 2. Of those that a mesh axis runs over, the one named last changes fastest.
Arguments:
- hidden: bfloat16 [32, 128, 28672], P('dp', None, 'tensor'), may hold values from -6 to 6
- out_grad: bfloat16 [32, 128, 8192], P('dp'), may hold values from -6 to 6
- w_down: bfloat16 [28672, 8192], P('tensor', 'dp'), may hold values from -0.0625 to 0.0625
- proj_in: bfloat16 [28672, 64], P('tensor'), may hold values from -0.03125 to 0.03125
- proj_out: bfloat16 [8192, 64], replicated, may hold values from -0.0625 to 0.0625
- queries: float32 [2048, 4096], P(('dp', 'tensor')), may hold values from -6 to 6
Outputs:
- back_grad: bfloat16 [32, 128, 28672], P('dp', None, 'tensor')
- scores: float32 [32, 2048], P(None, ('dp', 'tensor'))
The draws below stay inside these ranges and needn't reach their ends.
All inputs are finite; a program needn't handle non-finite values.
Results may differ from the reference program's by a relative error of at most 0.001.
Values may be sent and summed in bfloat16 or wider, within the bound.
No kernel may reach another device: no remote copies, remote signals or barrier semaphores. Data moves between devices by JAX's collectives and lax.ppermute only.
A program may use at most 128 MiB of HBM per device.

```python
import math
import jax
import jax.numpy as jnp
from jax import lax

D = 8192
FF = 28672
R = 64
SEQ = 128
EXAMPLES = 32
QUERIES = 2048


def block_levels(stream_key, shape, split, least, top_value):
    level, own = 1.0, jax.random.fold_in(stream_key, 6)
    for axis_at, shards_of in split:
        steps = jnp.exp(jax.random.uniform(jax.random.fold_in(own, axis_at), (shards_of,), jnp.float32, least / len(split), top_value / len(split)))
        level = level * jnp.repeat(steps, shape[axis_at] // shards_of).reshape([-1 if axis == axis_at else 1 for axis in range(len(shape))])
    return level


def scatter_about(key, shape, spread, limit, shards=(), dtype=jnp.bfloat16):
    drawn = jax.random.normal(key, shape, jnp.float32) * spread
    if len(shards) > 0:
        drawn = block_levels(key, shape, shards, -0.22, 0.18) * drawn
    return jnp.clip(drawn, min=-limit, max=limit).astype(dtype)


def setup_inputs(seed: int = 0) -> dict:
    splits = jax.random.split(jax.random.key(seed), 7)
    hidden = scatter_about(splits[0], (EXAMPLES, SEQ, FF), 1.0, 6.0, ((0, 16), (2, 16)))
    out_grad = scatter_about(splits[1], (EXAMPLES, SEQ, D), 1.0, 6.0, ((0, 16),))
    w_down = scatter_about(splits[2], (FF, D), D ** -0.5, 0.0625, ((0, 16), (1, 16)))
    proj_in = scatter_about(splits[3], (FF, R), FF ** -0.5, 0.03125, ((0, 16),))
    proj_out = scatter_about(splits[4], (D, R), D ** -0.5, 0.0625)
    queries = scatter_about(splits[5], (QUERIES, R * R), 1.0, 6.0, ((0, 256),), jnp.float32)
    return dict(hidden=hidden, out_grad=out_grad, w_down=w_down, proj_in=proj_in, proj_out=proj_out, queries=queries)


def reference(hidden, out_grad, w_down, proj_in, proj_out, queries):
    tok_rows = EXAMPLES * SEQ
    grads_flat = out_grad.reshape(tok_rows, D)
    back_sum = jnp.dot(grads_flat, w_down.T, preferred_element_type=jnp.float32)
    back_grad = back_sum.astype(jnp.bfloat16).reshape(EXAMPLES, SEQ, FF)
    inputs_proj = jnp.dot(hidden.reshape(tok_rows, FF), proj_in, preferred_element_type=jnp.float32)
    grads_proj = jnp.dot(grads_flat, proj_out, preferred_element_type=jnp.float32)
    features = jnp.einsum('esi,esj->eij', inputs_proj.reshape(EXAMPLES, SEQ, R), grads_proj.reshape(EXAMPLES, SEQ, R), precision=lax.Precision.HIGHEST)
    features = features.reshape(EXAMPLES, R * R)
    score_scale = 1.0 / (R * math.sqrt(SEQ))
    scores = jnp.dot(features, queries.T, precision=lax.Precision.HIGHEST) * score_scale
    return (back_grad, scores)
```

```python
import functools
import math

import jax
import jax.numpy as jnp
from jax import lax
from jax.experimental import pallas as pl
from jax.experimental.pallas import tpu as pltpu
from jax.sharding import PartitionSpec as P

XH, Z = 2, 8
XL, Y, C = 2, 4, 2
PIECES = Y * C
SPAN = 240.0
PAD = 16
VMEM = 48 * 1024 * 1024

Z_PERM = {
    r: [(i, (i // Z) * Z + (i + r) % Z) for i in range(XH * Z)] for r in range(-3, 5)
}
X_PERM = [(i, (i + Z) % (XH * Z)) for i in range(XH * Z)]
Y_PERM = {
    r: [(t, (t // PIECES) * PIECES + (t + r * C) % PIECES) for t in range(XL * Y * C)]
    for r in range(1, Y)
}
C_PERM = [(t, t ^ 1) for t in range(XL * Y * C)]


def nt_dot(a, b):
    return lax.dot_general(a, b, (((1,), (1,)), ((), ())), preferred_element_type=jnp.float32)


def own_sum(w_own, w_other, act):
    half = w_own.shape[1]
    return nt_dot(w_own, act[:, :half]) + nt_dot(w_other, act[:, half:])


def encode(out_ref, x):
    rows = x.shape[0]
    size = jnp.abs(x)
    top = jnp.maximum(jnp.max(size, axis=0, keepdims=True), 1e-30)
    scale = (top * 1.01).astype(jnp.bfloat16)
    level = size * (SPAN / scale.astype(jnp.float32)) - SPAN / 2
    code = jnp.exp2(level)
    out_ref[:rows, :] = jnp.where(x < 0, -code, code).astype(jnp.bfloat16)
    out_ref[rows:, :] = jnp.broadcast_to(scale, (PAD, x.shape[1]))


def decode(ref):
    rows = ref.shape[0] - PAD
    code = ref[:rows, :].astype(jnp.float32)
    unit = ref[rows : rows + 1, :].astype(jnp.float32) * (1.0 / SPAN)
    level = jnp.log(jnp.abs(code)) * (unit * (1.0 / math.log(2.0))) + unit * (SPAN / 2)
    return jnp.where(code < 0, -level, level)


def first_kernel(act, w_own, w_other, out):
    encode(out, own_sum(w_own[...], w_other[...], act[...]))


def next_kernel(act, w_own, w_other, came, out):
    encode(out, own_sum(w_own[...], w_other[...], act[...]) + decode(came))


def last_kernel(parts, act, w_own, w_other, *refs):
    came, out = refs[:-1], refs[-1]
    rows = came[0].shape[0] - PAD
    blocks = []
    for p in range(parts):
        at = slice(p * rows, (p + 1) * rows)
        x = own_sum(w_own[at, :], w_other[at, :], act[...])
        for c in came[p::parts]:
            x = x + decode(c)
        blocks.append(x)
    out[...] = jnp.concatenate(blocks, axis=0).T.astype(jnp.bfloat16)


def whole(x):
    return pl.BlockSpec(x.shape, lambda i: (0,) * x.ndim)


def step(act, w_down, w_other, chunk, at, came=None):
    toks, depth = act.shape
    args = [act, w_down, w_other] + ([] if came is None else [came])
    specs = [
        whole(act),
        pl.BlockSpec((chunk, depth // 2), lambda i: (at, 0)),
        pl.BlockSpec((chunk, depth // 2), lambda i: (at % 2, 0)),
    ] + ([] if came is None else [whole(came)])
    return pl.pallas_call(
        first_kernel if came is None else next_kernel,
        grid=(1,),
        in_specs=specs,
        out_specs=pl.BlockSpec((chunk + PAD, toks), lambda i: (0, 0)),
        out_shape=jax.ShapeDtypeStruct((chunk + PAD, toks), jnp.bfloat16),
        compiler_params=pltpu.CompilerParams(vmem_limit_bytes=VMEM),
        cost_estimate=pl.CostEstimate(
            flops=2 * chunk * toks * depth, bytes_accessed=2 * (chunk + toks) * depth, transcendentals=2 * chunk * toks
        ),
    )(*args)


def finish(act, w_down, w_other, chunk, group, came):
    toks, depth = act.shape
    rows = 2 * chunk
    return pl.pallas_call(
        functools.partial(last_kernel, 2),
        grid=(1,),
        in_specs=[
            whole(act),
            pl.BlockSpec((rows, depth // 2), lambda i: (group, 0)),
            pl.BlockSpec((rows, depth // 2), lambda i: (0, 0)),
        ]
        + [whole(c) for c in came],
        out_specs=pl.BlockSpec((toks, rows), lambda i: (0, 0)),
        out_shape=jax.ShapeDtypeStruct((toks, rows), jnp.bfloat16),
        compiler_params=pltpu.CompilerParams(vmem_limit_bytes=VMEM),
        cost_estimate=pl.CostEstimate(
            flops=2 * rows * toks * depth, bytes_accessed=2 * (rows + toks) * depth, transcendentals=2 * rows * toks
        ),
    )(act, w_down, w_other, *came)


def per_device(hidden, out_grad, w_down, proj_in, proj_out, queries):
    ex_dev, seq_len, ff_dev = hidden.shape
    model_width = out_grad.shape[2]
    toks = ex_dev * seq_len
    proj_rank = proj_in.shape[1]
    width = w_down.shape[1]
    grads_flat = out_grad.reshape(toks, model_width)
    hidden_flat = hidden.reshape(toks, ff_dev)
    dp, t = lax.axis_index("dp"), lax.axis_index("tensor")
    x_hi, z = dp // Z, dp % Z
    y = (t // C) % Y

    groups = 2
    chunk = ff_dev // (2 * groups)
    w_other = [
        lax.ppermute(w_down[g * 2 * chunk : (g + 1) * 2 * chunk], "dp", X_PERM) for g in range(groups)
    ]

    piece_rows = toks // PIECES
    mine = lax.dynamic_slice_in_dim(grads_flat, (t % PIECES) * piece_rows, piece_rows, 0)

    def columns(rows_of, z_at):
        own = lax.dynamic_slice_in_dim(rows_of, (x_hi * Z + z_at) * width, width, 1)
        other = lax.dynamic_slice_in_dim(rows_of, ((1 - x_hi) * Z + z_at) * width, width, 1)
        return jnp.concatenate([own, other], axis=1)

    acts = {}
    for offsets in ((4,), (3, -3), (2, -2, 1, -1)):
        got = jnp.stack(
            [lax.ppermute(columns(mine, (z - o) % Z), "dp", Z_PERM[-o if o < 4 else 4]) for o in offsets]
        )
        by_y = jnp.stack([got] + [lax.ppermute(got, "tensor", Y_PERM[Y - r]) for r in range(1, Y)], axis=1)
        other_core = lax.ppermute(by_y, "tensor", C_PERM)
        core0 = jnp.where(t % C == 0, by_y, other_core)
        core1 = jnp.where(t % C == 0, other_core, by_y)
        full = jnp.stack([core0, core1], axis=2).reshape(len(offsets), toks, 2 * width)
        for k, o in enumerate(offsets):
            acts[o] = full[k]
    turned = columns(grads_flat, z)
    y_rows = toks // Y
    acts[0] = lax.dynamic_slice_in_dim(jnp.concatenate([turned, turned], axis=0), y * y_rows, toks, 0)

    outs = []
    for g in range(groups):
        came = {}
        for n in range(4):
            for way in (1, -1):
                for part in (0, 1):
                    first = (part == 0) == (way == 1)
                    s = n if first else n - 1
                    o = (4 - n) if first else (4 - n)
                    if not first and n == 0:
                        continue
                    key = (way, part)
                    act = acts[o if (way == 1 or o == 4) else -o]
                    sent = step(act, w_down, w_other[g], chunk, 2 * g + part, came.get(key))
                    came[key] = lax.ppermute(sent, "dp", Z_PERM[way])
        outs.append(
            finish(
                acts[0], w_down, w_other[g], chunk, g, [came[(1, 0)], came[(1, 1)], came[(-1, 0)], came[(-1, 1)]]
            )
        )
    back = jnp.concatenate(outs, axis=1)
    back = lax.dynamic_slice_in_dim(
        jnp.concatenate([back, back], axis=0), ((Y - y) % Y) * y_rows, toks, 0
    )
    back_grad = back.reshape(ex_dev, seq_len, ff_dev)

    inputs_part = jnp.dot(hidden_flat, proj_in, preferred_element_type=jnp.float32)
    grads_proj = jnp.dot(grads_flat, proj_out, preferred_element_type=jnp.float32)
    part = jnp.einsum(
        "esi,esj->eij",
        inputs_part.reshape(ex_dev, seq_len, proj_rank),
        grads_proj.reshape(ex_dev, seq_len, proj_rank),
        precision=lax.Precision.HIGHEST,
    )
    devs_t = XL * Y * C
    cols = proj_rank * proj_rank // devs_t
    part = part.reshape(ex_dev, devs_t, cols).transpose(1, 0, 2)
    summed = lax.all_to_all(part, "tensor", 0, 0, tiled=True).sum(axis=0)
    devs_d = XH * Z
    over_dp = lax.all_to_all(
        jnp.broadcast_to(summed[None], (devs_d, ex_dev, cols)), "dp", 0, 0, tiled=True
    ).reshape(devs_d * ex_dev, cols)
    features = lax.all_to_all(
        jnp.broadcast_to(over_dp[None], (devs_t, devs_d * ex_dev, cols)), "tensor", 0, 0, tiled=True
    )
    features = features.transpose(1, 0, 2).reshape(devs_d * ex_dev, proj_rank * proj_rank)
    score_scale = 1.0 / (proj_rank * math.sqrt(seq_len))
    scores = jnp.dot(features, queries.T, precision=lax.Precision.HIGHEST) * score_scale
    return (back_grad, scores)


def solution(mesh):
    return jax.shard_map(
        per_device,
        mesh=mesh,
        in_specs=(
            P("dp", None, "tensor"),
            P("dp", None, None),
            P("tensor", "dp"),
            P("tensor", None),
            P(),
            P(("dp", "tensor"), None),
        ),
        out_specs=(P("dp", None, "tensor"), P(None, ("dp", "tensor"))),
        check_vma=False,
    )
```

```python
import functools
import math

import jax
import jax.numpy as jnp
from jax import lax
from jax.experimental import pallas as pl
from jax.experimental.pallas import tpu as pltpu
from jax.sharding import PartitionSpec as P

XH, Z = 2, 8
XL, Y, C = 2, 4, 2
PIECES = Y * C
SPAN = 240.0
PAD = 16
TILE = 128

Z_PERM = {
    r: [(i, (i // Z) * Z + (i + r) % Z) for i in range(XH * Z)] for r in range(-3, 5)
}
X_PERM = [(i, (i + Z) % (XH * Z)) for i in range(XH * Z)]
Y_PERM = {
    r: [(t, (t // PIECES) * PIECES + (t + r * C) % PIECES) for t in range(XL * Y * C)]
    for r in range(1, Y)
}
C_PERM = [(t, t ^ 1) for t in range(XL * Y * C)]
IN_VMEM = pl.BlockSpec(memory_space=pltpu.VMEM)
ANYWHERE = pl.BlockSpec(memory_space=pl.ANY)
LIMIT = 16 * 1024 * 1024


def nt_dot(a, b):
    return lax.dot_general(a, b, (((1,), (1,)), ((), ())), preferred_element_type=jnp.float32)


def encode(out, k, x):
    size = jnp.abs(x)
    top = jnp.maximum(jnp.max(size, axis=0, keepdims=True), 1e-30)
    scale = (top * 1.01).astype(jnp.bfloat16)
    level = size * (SPAN / scale.astype(jnp.float32)) - SPAN / 2
    code = jnp.exp2(level)
    out[k * TILE : (k + 1) * TILE, :] = jnp.where(x < 0, -code, code).astype(jnp.bfloat16)
    return scale


def decode(ref, scales, k):
    code = ref[k * TILE : (k + 1) * TILE, :].astype(jnp.float32)
    unit = scales[k : k + 1, :] * (1.0 / SPAN)
    level = jnp.log(jnp.abs(code)) * (unit * (1.0 / math.log(2.0))) + unit * (SPAN / 2)
    return jnp.where(code < 0, -level, level)


def scales_of(ref):
    rows = ref.shape[0] - PAD
    return ref[rows:, :].astype(jnp.float32)


def add_own(x, w_own, w_other, act):
    half = w_own.shape[1]
    x[...] = nt_dot(w_own[...], act[:, :half]) + nt_dot(w_other[...], act[:, half:])


def stage_kernel(at_r, at_l, part_r, n_in, n_after, mine, other, w_down, w_far, *refs):
    came = refs[:n_in]
    outs = refs[n_in + n_after : n_in + n_after + 2]
    x, acts, far, coming, sems = refs[n_in + n_after + 2 :]
    chunk = w_far.shape[0] // 2
    toks = x.shape[1]
    sides = ((at_r, part_r), (at_l, 1 - part_r))
    copies = []
    for side, (at, part) in enumerate(sides):
        rows = pl.ds(part * chunk, chunk)
        moves = [
            (mine.at[:, at], acts.at[side, :, 0]),
            (other.at[:, at], acts.at[side, :, 1]),
            (w_far.at[rows], far.at[side]),
        ]
        if n_in:
            moves.append((came[side], coming.at[side]))
        started = [pltpu.make_async_copy(src, dst, sems.at[side, k]) for k, (src, dst) in enumerate(moves)]
        for c in started:
            c.start()
        copies.append(started)
    for side, (_, part) in enumerate(sides):
        for c in copies[side]:
            c.wait()
        act = acts[side].reshape(toks, acts.shape[-1])
        add_own(x, w_down.at[pl.ds(part * chunk, chunk)], far.at[side], act)
        if n_in:
            scales = scales_of(coming.at[side])
        new = []
        for k in range(chunk // TILE):
            total = x[k * TILE : (k + 1) * TILE, :]
            if n_in:
                total = total + decode(coming.at[side], scales, k)
            new.append(encode(outs[side], k, total))
        new += [new[-1]] * (PAD - len(new))
        outs[side][chunk:, :] = jnp.concatenate(new, axis=0)


def own_kernel(starts_of, place, own, w_down, w_far, right, left, out):
    chunk = w_far.shape[0] // 2
    act = jnp.concatenate([own[pl.ds(s, n), :] for s, n in starts_of(place[0], place[1])], axis=0)
    for part, ref in ((0, left), (1, right)):
        rows = pl.ds(part * chunk, chunk)
        add_own(out.at[rows], w_down.at[rows], w_far.at[rows], act)
        scales = scales_of(ref)
        for k in range(chunk // TILE):
            at = slice(part * chunk + k * TILE, part * chunk + (k + 1) * TILE)
            out[at, :] = out[at, :] + decode(ref, scales, k)


def last_kernel(starts_of, place, before, right, left, out):
    chunk = before.shape[0] // 2
    starts = starts_of(place[0], place[1])
    for part, ref in ((0, right), (1, left)):
        scales = scales_of(ref)
        for k in range(chunk // TILE):
            row = part * chunk + k * TILE
            total = before[row : row + TILE, :] + decode(ref, scales, k)
            turned = total.T.astype(jnp.bfloat16)
            done = 0
            for s, n in starts:
                out[pl.ds(s, n), row : row + TILE] = turned[done : done + n, :]
                done += n


def pick_kernel(groups, z, planes, _, *outs):
    for offsets, out in zip(groups, outs):
        for k, o in enumerate(offsets):
            out[k] = planes[lax.rem(z[0] + (Z + o), Z)]


def pick(z, planes, groups, after):
    return pl.pallas_call(
        functools.partial(pick_kernel, groups),
        in_specs=[pl.BlockSpec(memory_space=pltpu.SMEM), IN_VMEM, ANYWHERE],
        out_specs=[IN_VMEM] * len(groups),
        out_shape=[jax.ShapeDtypeStruct((len(g), *planes.shape[1:]), planes.dtype) for g in groups],
    )(z.reshape(1).astype(jnp.int32), planes, after)


def cost(rows, toks, depth):
    return pl.CostEstimate(
        flops=2 * rows * toks * depth, bytes_accessed=rows * depth, transcendentals=2 * rows * toks
    )


def stage(at_r, at_l, part_r, mine, other, w_down, w_far, came, after):
    chunk, width = w_far.shape[0] // 2, w_far.shape[1]
    piece, depth = mine.shape[2:]
    toks = piece * PIECES
    coded = jax.ShapeDtypeStruct((chunk + PAD, toks), jnp.bfloat16)
    args = [mine, other, w_down, w_far, *came, *after]
    specs = [ANYWHERE] * len(args)
    specs[2] = IN_VMEM
    return pl.pallas_call(
        functools.partial(stage_kernel, at_r, at_l, part_r, len(came), len(after)),
        in_specs=specs,
        out_specs=[IN_VMEM] * 2,
        out_shape=[coded, coded],
        scratch_shapes=[
            pltpu.VMEM((chunk, toks), jnp.float32),
            pltpu.VMEM((2, Y, C, piece, depth), jnp.bfloat16),
            pltpu.VMEM((2, chunk, width), jnp.bfloat16),
            pltpu.VMEM((2, chunk + PAD, toks), jnp.bfloat16),
            pltpu.SemaphoreType.DMA((2, 4)),
        ],
        compiler_params=pltpu.CompilerParams(vmem_limit_bytes=LIMIT),
        cost_estimate=cost(2 * chunk, toks, depth),
    )(*args)


def starts_of(piece, y, core):
    starts = []
    for r in range(Y):
        for h in range(C):
            c = core if h == 0 else 1 - core
            starts.append((pl.multiple_of((lax.rem(y + r, Y) * C + c) * piece, piece), piece))
    return starts


def finish(place, own, w_down, w_far, early, late):
    toks = own.shape[0]
    rows = w_far.shape[0]
    find = functools.partial(starts_of, toks // PIECES)
    smem = pl.BlockSpec(memory_space=pltpu.SMEM)
    before = pl.pallas_call(
        functools.partial(own_kernel, find),
        in_specs=[smem] + [IN_VMEM] * 5,
        out_specs=IN_VMEM,
        out_shape=jax.ShapeDtypeStruct((rows, toks), jnp.float32),
        compiler_params=pltpu.CompilerParams(vmem_limit_bytes=LIMIT),
        cost_estimate=cost(rows, toks, own.shape[1]),
    )(place, own, w_down, w_far, *early)
    return pl.pallas_call(
        functools.partial(last_kernel, find),
        in_specs=[smem] + [IN_VMEM] * 3,
        out_specs=IN_VMEM,
        out_shape=jax.ShapeDtypeStruct((toks, rows), jnp.bfloat16),
        compiler_params=pltpu.CompilerParams(vmem_limit_bytes=LIMIT),
        cost_estimate=cost(rows, toks, 0),
    )(place, before, *late)


def per_device(hidden, out_grad, w_down, proj_in, proj_out, queries):
    ex_dev, seq_len, ff_dev = hidden.shape
    model_width = out_grad.shape[2]
    toks = ex_dev * seq_len
    proj_rank = proj_in.shape[1]
    width = w_down.shape[1]
    grads_flat = out_grad.reshape(toks, model_width)
    hidden_flat = hidden.reshape(toks, ff_dev)
    dp, t = lax.axis_index("dp"), lax.axis_index("tensor")
    x_hi, z = dp // Z, dp % Z

    w_far = lax.ppermute(w_down, "dp", X_PERM)

    piece_rows = toks // PIECES
    own_rows = lax.dynamic_slice_in_dim(grads_flat, (t % PIECES) * piece_rows, piece_rows, 0)

    def columns(rows_of):
        rows = rows_of.shape[0]
        split = rows_of.reshape(rows, XH, Z, width)
        own = lax.dynamic_index_in_dim(split, x_hi, 1, keepdims=False)
        other = lax.dynamic_index_in_dim(split, 1 - x_hi, 1, keepdims=False)
        return jnp.concatenate([own, other], axis=2).transpose(1, 0, 2)

    rings = [list(range(h * Z, (h + 1) * Z)) for h in range(XH)]
    planes = lax.all_to_all(columns(own_rows), "dp", 0, 0, axis_index_groups=rings, tiled=True)

    inputs_part = jnp.dot(hidden_flat, proj_in, preferred_element_type=jnp.float32)
    grads_proj = jnp.dot(grads_flat, proj_out, preferred_element_type=jnp.float32)
    part = jnp.einsum(
        "esi,esj->eij",
        inputs_part.reshape(ex_dev, seq_len, proj_rank),
        grads_proj.reshape(ex_dev, seq_len, proj_rank),
        precision=lax.Precision.HIGHEST,
    )
    devs_t, devs_d = XL * Y * C, XH * Z
    cols = proj_rank * proj_rank // devs_t
    part = part.reshape(ex_dev, devs_t, cols).transpose(1, 0, 2)
    summed = lax.all_to_all(part, "tensor", 0, 0, tiled=True).sum(axis=0)

    groups = ((4, 3, -3), (2, -2, 1, -1))
    acts = {}
    for offsets, got in zip(groups, pick(z, planes, groups, part)):
        mine = jnp.stack([got] + [lax.ppermute(got, "tensor", Y_PERM[Y - r]) for r in range(1, Y)])
        other = lax.ppermute(mine, "tensor", C_PERM)
        for k, o in enumerate(offsets):
            acts[o] = (k, mine, other)

    over_z = lax.all_to_all(
        jnp.broadcast_to(summed[None], (Z, ex_dev, cols)), "dp", 0, 0, axis_index_groups=rings, tiled=True
    ).reshape(Z * ex_dev, cols)
    over_x = lax.ppermute(over_z, "dp", X_PERM)
    first = x_hi == 0
    over_dp = jnp.concatenate([jnp.where(first, over_z, over_x), jnp.where(first, over_x, over_z)], axis=0)
    features = lax.all_to_all(
        jnp.broadcast_to(over_dp[None], (devs_t, devs_d * ex_dev, cols)), "tensor", 0, 0, tiled=True
    )

    came = {}
    for s in range(7):
        hops = 4 - (s + 1) // 2
        part_r = s % 2
        at_r, mine, other = acts[hops]
        at_l = acts[hops if hops == 4 else -hops][0]
        before = came.get(s - 2, [])
        right, left = stage(
            at_r, at_l, part_r, mine, other, w_down, w_far, before, [over_z if s == 0 else right]
        )
        came[s] = [lax.ppermute(right, "dp", Z_PERM[1]), lax.ppermute(left, "dp", Z_PERM[-1])]
    own_act = jnp.concatenate(
        [
            lax.dynamic_slice_in_dim(grads_flat, (h * Z + z) * width, width, 1)
            for h in (x_hi, 1 - x_hi)
        ],
        axis=1,
    )
    back = finish(jnp.stack([(t // C) % Y, t % C]).astype(jnp.int32), own_act, w_down, w_far, came[5], came[6])
    back_grad = back.reshape(ex_dev, seq_len, ff_dev)

    features = features.transpose(1, 0, 2).reshape(devs_d * ex_dev, proj_rank * proj_rank)
    score_scale = 1.0 / (proj_rank * math.sqrt(seq_len))
    scores = jnp.dot(features, queries.T, precision=lax.Precision.HIGHEST) * score_scale
    return (back_grad, scores)


def solution(mesh):
    return jax.shard_map(
        per_device,
        mesh=mesh,
        in_specs=(
            P("dp", None, "tensor"),
            P("dp", None, None),
            P("tensor", "dp"),
            P("tensor", None),
            P(),
            P(("dp", "tensor"), None),
        ),
        out_specs=(P("dp", None, "tensor"), P(None, ("dp", "tensor"))),
        check_vma=False,
    )
```

```python
import functools
import math

import jax
import jax.numpy as jnp
from jax import lax
from jax.experimental import pallas as pl
from jax.experimental.pallas import tpu as pltpu
from jax.sharding import PartitionSpec as P

XH, Z = 2, 8
XL, Y, C = 2, 4, 2
PIECES = Y * C
SPAN = 240.0
PAD = 16
TILE = 128

Z_PERM = {
    r: [(i, (i // Z) * Z + (i + r) % Z) for i in range(XH * Z)] for r in range(-3, 5)
}
X_PERM = [(i, (i + Z) % (XH * Z)) for i in range(XH * Z)]
Y_PERM = {
    r: [(t, (t // PIECES) * PIECES + (t + r * C) % PIECES) for t in range(XL * Y * C)]
    for r in range(1, Y)
}
C_PERM = [(t, t ^ 1) for t in range(XL * Y * C)]
IN_VMEM = pl.BlockSpec(memory_space=pltpu.VMEM)
ANYWHERE = pl.BlockSpec(memory_space=pl.ANY)
LIMIT = 16 * 1024 * 1024


def nt_dot(a, b):
    return lax.dot_general(a, b, (((1,), (1,)), ((), ())), preferred_element_type=jnp.float32)


def encode(out, k, x):
    size = jnp.abs(x)
    top = jnp.maximum(jnp.max(size, axis=0, keepdims=True), 1e-30)
    scale = (top * 1.01).astype(jnp.bfloat16)
    level = size * (SPAN / scale.astype(jnp.float32)) - SPAN / 2
    code = jnp.exp2(level)
    out[k * TILE : (k + 1) * TILE, :] = jnp.where(x < 0, -code, code).astype(jnp.bfloat16)
    return scale


def decode(ref, scales, k):
    code = ref[k * TILE : (k + 1) * TILE, :].astype(jnp.float32)
    unit = scales[k : k + 1, :] * (1.0 / SPAN)
    level = jnp.log(jnp.abs(code)) * (unit * (1.0 / math.log(2.0))) + unit * (SPAN / 2)
    return jnp.where(code < 0, -level, level)


def scales_of(ref):
    rows = ref.shape[0] - PAD
    return ref[rows:, :].astype(jnp.float32)


def add_own(x, w_own, w_other, act):
    half = w_own.shape[1]
    x[...] = nt_dot(w_own[...], act[:, :half]) + nt_dot(w_other[...], act[:, half:])


def stage_kernel(at_r, at_l, part_r, n_in, n_after, mine, other, w_down, w_far, *refs):
    came = refs[:n_in]
    outs = refs[n_in + n_after : n_in + n_after + 2]
    x, acts, far, coming, sems = refs[n_in + n_after + 2 :]
    chunk = w_far.shape[0] // 2
    toks = x.shape[1]
    sides = ((at_r, part_r), (at_l, 1 - part_r))
    copies = []
    for side, (at, part) in enumerate(sides):
        rows = pl.ds(part * chunk, chunk)
        moves = [
            (mine.at[:, at], acts.at[side, :, 0]),
            (other.at[:, at], acts.at[side, :, 1]),
            (w_far.at[rows], far.at[side]),
        ]
        if n_in:
            moves.append((came[side], coming.at[side]))
        started = [pltpu.make_async_copy(src, dst, sems.at[side, k]) for k, (src, dst) in enumerate(moves)]
        copies.append(started)
    for c in copies[0]:
        c.start()
    for side, (_, part) in enumerate(sides):
        for c in copies[side]:
            c.wait()
        if side == 0:
            for c in copies[1]:
                c.start()
        act = acts[side].reshape(toks, acts.shape[-1])
        add_own(x, w_down.at[pl.ds(part * chunk, chunk)], far.at[side], act)
        if n_in:
            scales = scales_of(coming.at[side])
        new = []
        for k in range(chunk // TILE):
            total = x[k * TILE : (k + 1) * TILE, :]
            if n_in:
                total = total + decode(coming.at[side], scales, k)
            new.append(encode(outs[side], k, total))
        new += [new[-1]] * (PAD - len(new))
        outs[side][chunk:, :] = jnp.concatenate(new, axis=0)


def own_kernel(starts_of, place, own, w_down, w_far, right, left, out):
    chunk = w_far.shape[0] // 2
    act = jnp.concatenate([own[pl.ds(s, n), :] for s, n in starts_of(place[0], place[1])], axis=0)
    for part, ref in ((0, left), (1, right)):
        rows = pl.ds(part * chunk, chunk)
        add_own(out.at[rows], w_down.at[rows], w_far.at[rows], act)
        scales = scales_of(ref)
        for k in range(chunk // TILE):
            at = slice(part * chunk + k * TILE, part * chunk + (k + 1) * TILE)
            out[at, :] = out[at, :] + decode(ref, scales, k)


def last_kernel(starts_of, place, before, right, left, out):
    chunk = before.shape[0] // 2
    starts = starts_of(place[0], place[1])
    for part, ref in ((0, right), (1, left)):
        scales = scales_of(ref)
        for k in range(chunk // TILE):
            row = part * chunk + k * TILE
            total = before[row : row + TILE, :] + decode(ref, scales, k)
            turned = total.T.astype(jnp.bfloat16)
            done = 0
            for s, n in starts:
                out[pl.ds(s, n), row : row + TILE] = turned[done : done + n, :]
                done += n


def pick_kernel(groups, z, planes, _, *outs):
    for offsets, out in zip(groups, outs):
        for k, o in enumerate(offsets):
            out[k] = planes[lax.rem(z[0] + (Z + o), Z)]


def pick(z, planes, groups, after):
    return pl.pallas_call(
        functools.partial(pick_kernel, groups),
        in_specs=[pl.BlockSpec(memory_space=pltpu.SMEM), IN_VMEM, ANYWHERE],
        out_specs=[IN_VMEM] * len(groups),
        out_shape=[jax.ShapeDtypeStruct((len(g), *planes.shape[1:]), planes.dtype) for g in groups],
    )(z.reshape(1).astype(jnp.int32), planes, after)


def cost(rows, toks, depth):
    return pl.CostEstimate(
        flops=2 * rows * toks * depth, bytes_accessed=rows * depth, transcendentals=2 * rows * toks
    )


def stage(at_r, at_l, part_r, mine, other, w_down, w_far, came, after):
    chunk, width = w_far.shape[0] // 2, w_far.shape[1]
    piece, depth = mine.shape[2:]
    toks = piece * PIECES
    coded = jax.ShapeDtypeStruct((chunk + PAD, toks), jnp.bfloat16)
    args = [mine, other, w_down, w_far, *came, *after]
    specs = [ANYWHERE] * len(args)
    specs[2] = IN_VMEM
    return pl.pallas_call(
        functools.partial(stage_kernel, at_r, at_l, part_r, len(came), len(after)),
        in_specs=specs,
        out_specs=[IN_VMEM] * 2,
        out_shape=[coded, coded],
        scratch_shapes=[
            pltpu.VMEM((chunk, toks), jnp.float32),
            pltpu.VMEM((2, Y, C, piece, depth), jnp.bfloat16),
            pltpu.VMEM((2, chunk, width), jnp.bfloat16),
            pltpu.VMEM((2, chunk + PAD, toks), jnp.bfloat16),
            pltpu.SemaphoreType.DMA((2, 4)),
        ],
        compiler_params=pltpu.CompilerParams(vmem_limit_bytes=LIMIT),
        cost_estimate=cost(2 * chunk, toks, depth),
    )(*args)


def starts_of(piece, y, core):
    starts = []
    for r in range(Y):
        for h in range(C):
            c = core if h == 0 else 1 - core
            starts.append((pl.multiple_of((lax.rem(y + r, Y) * C + c) * piece, piece), piece))
    return starts


def finish(place, own, w_down, w_far, early, late):
    toks = own.shape[0]
    rows = w_far.shape[0]
    find = functools.partial(starts_of, toks // PIECES)
    smem = pl.BlockSpec(memory_space=pltpu.SMEM)
    before = pl.pallas_call(
        functools.partial(own_kernel, find),
        in_specs=[smem] + [IN_VMEM] * 5,
        out_specs=IN_VMEM,
        out_shape=jax.ShapeDtypeStruct((rows, toks), jnp.float32),
        compiler_params=pltpu.CompilerParams(vmem_limit_bytes=LIMIT),
        cost_estimate=cost(rows, toks, own.shape[1]),
    )(place, own, w_down, w_far, *early)
    return pl.pallas_call(
        functools.partial(last_kernel, find),
        in_specs=[smem] + [IN_VMEM] * 3,
        out_specs=IN_VMEM,
        out_shape=jax.ShapeDtypeStruct((toks, rows), jnp.bfloat16),
        compiler_params=pltpu.CompilerParams(vmem_limit_bytes=LIMIT),
        cost_estimate=cost(rows, toks, 0),
    )(place, before, *late)


def per_device(hidden, out_grad, w_down, proj_in, proj_out, queries):
    ex_dev, seq_len, ff_dev = hidden.shape
    model_width = out_grad.shape[2]
    toks = ex_dev * seq_len
    proj_rank = proj_in.shape[1]
    width = w_down.shape[1]
    grads_flat = out_grad.reshape(toks, model_width)
    hidden_flat = hidden.reshape(toks, ff_dev)
    dp, t = lax.axis_index("dp"), lax.axis_index("tensor")
    x_hi, z = dp // Z, dp % Z

    w_far = lax.ppermute(w_down, "dp", X_PERM)

    piece_rows = toks // PIECES
    own_rows = lax.dynamic_slice_in_dim(grads_flat, (t % PIECES) * piece_rows, piece_rows, 0)

    def columns(rows_of):
        rows = rows_of.shape[0]
        split = rows_of.reshape(rows, XH, Z, width)
        own = lax.dynamic_index_in_dim(split, x_hi, 1, keepdims=False)
        other = lax.dynamic_index_in_dim(split, 1 - x_hi, 1, keepdims=False)
        return jnp.concatenate([own, other], axis=2).transpose(1, 0, 2)

    rings = [list(range(h * Z, (h + 1) * Z)) for h in range(XH)]
    planes = lax.all_to_all(columns(own_rows), "dp", 0, 0, axis_index_groups=rings, tiled=True)

    inputs_part = jnp.dot(hidden_flat, proj_in, preferred_element_type=jnp.float32)
    grads_proj = jnp.dot(grads_flat, proj_out, preferred_element_type=jnp.float32)
    part = jnp.einsum(
        "esi,esj->eij",
        inputs_part.reshape(ex_dev, seq_len, proj_rank),
        grads_proj.reshape(ex_dev, seq_len, proj_rank),
        precision=lax.Precision.HIGHEST,
    )
    devs_t, devs_d = XL * Y * C, XH * Z
    cols = proj_rank * proj_rank // devs_t
    part = part.reshape(ex_dev, devs_t, cols).transpose(1, 0, 2)
    summed = lax.all_to_all(part, "tensor", 0, 0, tiled=True).sum(axis=0)

    groups = ((4, 3, -3), (2, -2, 1, -1))
    acts = {}
    for offsets, got in zip(groups, pick(z, planes, groups, part)):
        mine = jnp.stack([got] + [lax.ppermute(got, "tensor", Y_PERM[Y - r]) for r in range(1, Y)])
        other = lax.ppermute(mine, "tensor", C_PERM)
        for k, o in enumerate(offsets):
            acts[o] = (k, mine, other)

    over_z = lax.all_to_all(
        jnp.broadcast_to(summed[None], (Z, ex_dev, cols)), "dp", 0, 0, axis_index_groups=rings, tiled=True
    ).reshape(Z * ex_dev, cols)
    over_x = lax.ppermute(over_z, "dp", X_PERM)
    first = x_hi == 0
    over_dp = jnp.concatenate([jnp.where(first, over_z, over_x), jnp.where(first, over_x, over_z)], axis=0)
    features = lax.all_to_all(
        jnp.broadcast_to(over_dp[None], (devs_t, devs_d * ex_dev, cols)), "tensor", 0, 0, tiled=True
    )

    came = {}
    for s in range(7):
        hops = 4 - (s + 1) // 2
        part_r = s % 2
        at_r, mine, other = acts[hops]
        at_l = acts[hops if hops == 4 else -hops][0]
        before = came.get(s - 2, [])
        right, left = stage(
            at_r, at_l, part_r, mine, other, w_down, w_far, before, [over_z if s == 0 else right]
        )
        came[s] = [lax.ppermute(right, "dp", Z_PERM[1]), lax.ppermute(left, "dp", Z_PERM[-1])]
    own_act = jnp.concatenate(
        [
            lax.dynamic_slice_in_dim(grads_flat, (h * Z + z) * width, width, 1)
            for h in (x_hi, 1 - x_hi)
        ],
        axis=1,
    )
    back = finish(jnp.stack([(t // C) % Y, t % C]).astype(jnp.int32), own_act, w_down, w_far, came[5], came[6])
    back_grad = back.reshape(ex_dev, seq_len, ff_dev)

    features = features.transpose(1, 0, 2).reshape(devs_d * ex_dev, proj_rank * proj_rank)
    score_scale = 1.0 / (proj_rank * math.sqrt(seq_len))
    scores = jnp.dot(features, queries.T, precision=lax.Precision.HIGHEST) * score_scale
    return (back_grad, scores)


def solution(mesh):
    return jax.shard_map(
        per_device,
        mesh=mesh,
        in_specs=(
            P("dp", None, "tensor"),
            P("dp", None, None),
            P("tensor", "dp"),
            P("tensor", None),
            P(),
            P(("dp", "tensor"), None),
        ),
        out_specs=(P("dp", None, "tensor"), P(None, ("dp", "tensor"))),
        check_vma=False,
    )
```

```python
import functools
import math

import jax
import jax.numpy as jnp
from jax import lax
from jax.experimental import pallas as pl
from jax.experimental.pallas import tpu as pltpu
from jax.sharding import PartitionSpec as P

XH, Z = 2, 8
XL, Y, C = 2, 4, 2
PIECES = Y * C
SPAN = 240.0
PAD = 16
TILE = 128

Z_PERM = {
    r: [(i, (i // Z) * Z + (i + r) % Z) for i in range(XH * Z)] for r in range(-3, 5)
}
X_PERM = [(i, (i + Z) % (XH * Z)) for i in range(XH * Z)]
Y_PERM = {
    r: [(t, (t // PIECES) * PIECES + (t + r * C) % PIECES) for t in range(XL * Y * C)]
    for r in range(1, Y)
}
C_PERM = [(t, t ^ 1) for t in range(XL * Y * C)]
IN_VMEM = pl.BlockSpec(memory_space=pltpu.VMEM)
ANYWHERE = pl.BlockSpec(memory_space=pl.ANY)
LIMIT = 16 * 1024 * 1024


def nt_dot(a, b):
    return lax.dot_general(a, b, (((1,), (1,)), ((), ())), preferred_element_type=jnp.float32)


def encode(out, k, x):
    size = jnp.abs(x)
    top = jnp.maximum(jnp.max(size, axis=0, keepdims=True), 1e-30)
    scale = (top * 1.01).astype(jnp.bfloat16)
    level = size * (SPAN / scale.astype(jnp.float32)) - SPAN / 2
    code = jnp.exp2(level)
    out[k * TILE : (k + 1) * TILE, :] = jnp.where(x < 0, -code, code).astype(jnp.bfloat16)
    return scale


def decode(ref, scales, k):
    code = ref[k * TILE : (k + 1) * TILE, :].astype(jnp.float32)
    unit = scales[k : k + 1, :] * (1.0 / SPAN)
    level = jnp.log(jnp.abs(code)) * (unit * (1.0 / math.log(2.0))) + unit * (SPAN / 2)
    return jnp.where(code < 0, -level, level)


def scales_of(ref):
    rows = ref.shape[0] - PAD
    return ref[rows:, :].astype(jnp.float32)


def add_own(x, w_own, w_other, act):
    half = w_own.shape[1]
    x[...] = nt_dot(w_own[...], act[:, :half]) + nt_dot(w_other[...], act[:, half:])


def stage_kernel(at_r, at_l, part_r, n_in, n_after, mine, other, w_down, w_far, *refs):
    came = refs[:n_in]
    outs = refs[n_in + n_after : n_in + n_after + 2]
    x, acts, far, coming, sems = refs[n_in + n_after + 2 :]
    chunk = w_far.shape[0] // 2
    toks = x.shape[1]
    sides = ((at_r, part_r), (at_l, 1 - part_r))
    copies = []
    for side, (at, part) in enumerate(sides):
        rows = pl.ds(part * chunk, chunk)
        moves = [
            (mine.at[:, at], acts.at[side, :, 0]),
            (other.at[:, at], acts.at[side, :, 1]),
            (w_far.at[rows], far.at[side]),
        ]
        if n_in:
            moves.append((came[side], coming.at[side]))
        started = [pltpu.make_async_copy(src, dst, sems.at[side, k]) for k, (src, dst) in enumerate(moves)]
        for c in started:
            c.start()
        copies.append(started)
    for side, (_, part) in enumerate(sides):
        for c in copies[side]:
            c.wait()
        act = acts[side].reshape(toks, acts.shape[-1])
        add_own(x, w_down.at[pl.ds(part * chunk, chunk)], far.at[side], act)
        if n_in:
            scales = scales_of(coming.at[side])
        new = []
        for k in range(chunk // TILE):
            total = x[k * TILE : (k + 1) * TILE, :]
            if n_in:
                total = total + decode(coming.at[side], scales, k)
            new.append(encode(outs[side], k, total))
        new += [new[-1]] * (PAD - len(new))
        outs[side][chunk:, :] = jnp.concatenate(new, axis=0)


def own_kernel(starts_of, place, own, w_down, w_far, right, left, out):
    chunk = w_far.shape[0] // 2
    act = jnp.concatenate([own[pl.ds(s, n), :] for s, n in starts_of(place[0], place[1])], axis=0)
    for part, ref in ((0, left), (1, right)):
        rows = pl.ds(part * chunk, chunk)
        add_own(out.at[rows], w_down.at[rows], w_far.at[rows], act)
        scales = scales_of(ref)
        for k in range(chunk // TILE):
            at = slice(part * chunk + k * TILE, part * chunk + (k + 1) * TILE)
            out[at, :] = out[at, :] + decode(ref, scales, k)


def last_kernel(starts_of, place, before, right, left, out):
    chunk = before.shape[0] // 2
    starts = starts_of(place[0], place[1])
    for part, ref in ((0, right), (1, left)):
        scales = scales_of(ref)
        for k in range(chunk // TILE):
            row = part * chunk + k * TILE
            total = before[row : row + TILE, :] + decode(ref, scales, k)
            turned = total.T.astype(jnp.bfloat16)
            done = 0
            for s, n in starts:
                out[pl.ds(s, n), row : row + TILE] = turned[done : done + n, :]
                done += n


def pick_kernel(groups, z, planes, _, *outs):
    for offsets, out in zip(groups, outs):
        for k, o in enumerate(offsets):
            out[k] = planes[lax.rem(z[0] + (Z + o), Z)]


def pick(z, planes, groups, after):
    return pl.pallas_call(
        functools.partial(pick_kernel, groups),
        in_specs=[pl.BlockSpec(memory_space=pltpu.SMEM), IN_VMEM, ANYWHERE],
        out_specs=[IN_VMEM] * len(groups),
        out_shape=[jax.ShapeDtypeStruct((len(g), *planes.shape[1:]), planes.dtype) for g in groups],
    )(z.reshape(1).astype(jnp.int32), planes, after)


def cost(rows, toks, depth):
    return pl.CostEstimate(
        flops=2 * rows * toks * depth, bytes_accessed=rows * depth, transcendentals=2 * rows * toks
    )


def stage(at_r, at_l, part_r, mine, other, w_down, w_far, came, after):
    chunk, width = w_far.shape[0] // 2, w_far.shape[1]
    piece, depth = mine.shape[2:]
    toks = piece * PIECES
    coded = jax.ShapeDtypeStruct((chunk + PAD, toks), jnp.bfloat16)
    args = [mine, other, w_down, w_far, *came, *after]
    specs = [ANYWHERE] * len(args)
    specs[2] = IN_VMEM
    return pl.pallas_call(
        functools.partial(stage_kernel, at_r, at_l, part_r, len(came), len(after)),
        in_specs=specs,
        out_specs=[IN_VMEM] * 2,
        out_shape=[coded, coded],
        scratch_shapes=[
            pltpu.VMEM((chunk, toks), jnp.float32),
            pltpu.VMEM((2, Y, C, piece, depth), jnp.bfloat16),
            pltpu.VMEM((2, chunk, width), jnp.bfloat16),
            pltpu.VMEM((2, chunk + PAD, toks), jnp.bfloat16),
            pltpu.SemaphoreType.DMA((2, 4)),
        ],
        compiler_params=pltpu.CompilerParams(vmem_limit_bytes=LIMIT),
        cost_estimate=cost(2 * chunk, toks, depth),
    )(*args)


def starts_of(piece, y, core):
    starts = []
    for r in range(Y):
        for h in range(C):
            c = core if h == 0 else 1 - core
            starts.append((pl.multiple_of((lax.rem(y + r, Y) * C + c) * piece, piece), piece))
    return starts


def finish(place, own, w_down, w_far, early, late):
    toks = own.shape[0]
    rows = w_far.shape[0]
    find = functools.partial(starts_of, toks // PIECES)
    smem = pl.BlockSpec(memory_space=pltpu.SMEM)
    before = pl.pallas_call(
        functools.partial(own_kernel, find),
        in_specs=[smem] + [IN_VMEM] * 5,
        out_specs=IN_VMEM,
        out_shape=jax.ShapeDtypeStruct((rows, toks), jnp.float32),
        compiler_params=pltpu.CompilerParams(vmem_limit_bytes=LIMIT),
        cost_estimate=cost(rows, toks, own.shape[1]),
    )(place, own, w_down, w_far, *early)
    return pl.pallas_call(
        functools.partial(last_kernel, find),
        in_specs=[smem] + [IN_VMEM] * 3,
        out_specs=IN_VMEM,
        out_shape=jax.ShapeDtypeStruct((toks, rows), jnp.bfloat16),
        compiler_params=pltpu.CompilerParams(vmem_limit_bytes=LIMIT),
        cost_estimate=cost(rows, toks, 0),
    )(place, before, *late)


def per_device(hidden, out_grad, w_down, proj_in, proj_out, queries):
    ex_dev, seq_len, ff_dev = hidden.shape
    model_width = out_grad.shape[2]
    toks = ex_dev * seq_len
    proj_rank = proj_in.shape[1]
    width = w_down.shape[1]
    grads_flat = out_grad.reshape(toks, model_width)
    hidden_flat = hidden.reshape(toks, ff_dev)
    dp, t = lax.axis_index("dp"), lax.axis_index("tensor")
    x_hi, z = dp // Z, dp % Z

    w_far = lax.ppermute(w_down, "dp", X_PERM)

    piece_rows = toks // PIECES
    own_rows = lax.dynamic_slice_in_dim(grads_flat, (t % PIECES) * piece_rows, piece_rows, 0)

    def columns(rows_of):
        rows = rows_of.shape[0]
        split = rows_of.reshape(rows, XH, Z, width)
        own = lax.dynamic_index_in_dim(split, x_hi, 1, keepdims=False)
        other = lax.dynamic_index_in_dim(split, 1 - x_hi, 1, keepdims=False)
        return jnp.concatenate([own, other], axis=2).transpose(1, 0, 2)

    rings = [list(range(h * Z, (h + 1) * Z)) for h in range(XH)]
    planes = lax.all_to_all(columns(own_rows), "dp", 0, 0, axis_index_groups=rings, tiled=True)

    inputs_part = jnp.dot(hidden_flat, proj_in, preferred_element_type=jnp.float32)
    grads_proj = jnp.dot(grads_flat, proj_out, preferred_element_type=jnp.float32)
    part = jnp.einsum(
        "esi,esj->eij",
        inputs_part.reshape(ex_dev, seq_len, proj_rank),
        grads_proj.reshape(ex_dev, seq_len, proj_rank),
        precision=lax.Precision.HIGHEST,
    )
    devs_t, devs_d = XL * Y * C, XH * Z
    cols = proj_rank * proj_rank // PIECES
    planes_yc = [list(range(h * PIECES, (h + 1) * PIECES)) for h in range(XL)]
    part = part.reshape(ex_dev, PIECES, cols).transpose(1, 0, 2)
    summed = lax.all_to_all(part, "tensor", 0, 0, axis_index_groups=planes_yc, tiled=True).sum(axis=0)

    groups = ((4, 3, -3), (2, -2, 1, -1))
    acts = {}
    for offsets, got in zip(groups, pick(z, planes, groups, part)):
        mine = jnp.stack([got] + [lax.ppermute(got, "tensor", Y_PERM[Y - r]) for r in range(1, Y)])
        other = lax.ppermute(mine, "tensor", C_PERM)
        for k, o in enumerate(offsets):
            acts[o] = (k, mine, other)

    over_z = lax.all_to_all(
        jnp.broadcast_to(summed[None], (Z, ex_dev, cols)), "dp", 0, 0, axis_index_groups=rings, tiled=True
    ).reshape(Z * ex_dev, cols)
    over_x = lax.ppermute(over_z, "dp", X_PERM)
    first = x_hi == 0
    over_dp = jnp.concatenate([jnp.where(first, over_z, over_x), jnp.where(first, over_x, over_z)], axis=0)
    features = lax.all_to_all(
        jnp.broadcast_to(over_dp[None], (devs_t, devs_d * ex_dev, cols)), "tensor", 0, 0, tiled=True
    )

    came = {}
    for s in range(7):
        hops = 4 - (s + 1) // 2
        part_r = s % 2
        at_r, mine, other = acts[hops]
        at_l = acts[hops if hops == 4 else -hops][0]
        before = came.get(s - 2, [])
        right, left = stage(
            at_r, at_l, part_r, mine, other, w_down, w_far, before, [over_z if s == 0 else right]
        )
        came[s] = [lax.ppermute(right, "dp", Z_PERM[1]), lax.ppermute(left, "dp", Z_PERM[-1])]
    own_act = jnp.concatenate(
        [
            lax.dynamic_slice_in_dim(grads_flat, (h * Z + z) * width, width, 1)
            for h in (x_hi, 1 - x_hi)
        ],
        axis=1,
    )
    back = finish(jnp.stack([(t // C) % Y, t % C]).astype(jnp.int32), own_act, w_down, w_far, came[5], came[6])
    back_grad = back.reshape(ex_dev, seq_len, ff_dev)

    features = features.reshape(XL, PIECES, devs_d * ex_dev, cols).sum(axis=0)
    features = features.transpose(1, 0, 2).reshape(devs_d * ex_dev, proj_rank * proj_rank)
    score_scale = 1.0 / (proj_rank * math.sqrt(seq_len))
    scores = jnp.dot(features, queries.T, precision=lax.Precision.HIGHEST) * score_scale
    return (back_grad, scores)


def solution(mesh):
    return jax.shard_map(
        per_device,
        mesh=mesh,
        in_specs=(
            P("dp", None, "tensor"),
            P("dp", None, None),
            P("tensor", "dp"),
            P("tensor", None),
            P(),
            P(("dp", "tensor"), None),
        ),
        out_specs=(P("dp", None, "tensor"), P(None, ("dp", "tensor"))),
        check_vma=False,
    )
```
